256 devices in a mesh: sfc: 64 (over y, z, core), aux: 4 (over x).
Axes of the slice: x: 4, y: 4, z: 8, core: 2. Of those that a mesh axis runs over, the one named last changes fastest.
Arguments:
- three_index: bfloat16 [128, 4, 160, 128, 128], P('sfc', None, 'aux'), may hold values from -0.14941406 to 0.14941406
- density: bfloat16 [128, 13, 128, 128], P('sfc'), may hold values from -6 to 6
- neighbours: int32 [128, 4], P('sfc'), may hold values from 0 to 127, as said below
- partner: int32 [128, 4], P('sfc'), may hold values from 0 to 3
- block_mask: int32 [128, 4], P('sfc'), may hold values 0 or 1
Outputs:
- exchange: float32 [128, 13, 128, 128], P('sfc', None, 'aux')
The draws below stay inside these ranges and needn't reach their ends.
Inputs may be any that keep to these rules, and one draw needn't show every extreme that they name: neighbours[g, 0] is g; the entries of a row are distinct groups (g + s) mod 128 with s between -3 and 3.
All inputs are finite; a program needn't handle non-finite values. No bound on the sum of `block_mask` on one device may be relied on, other than what follows from the above.
Results may differ from the reference program's by a relative error of at most 0.0029.
Values may be sent and summed in bfloat16 or wider, within the bound.
No kernel may reach another device: no remote copies, remote signals or barrier semaphores. Data moves between devices by JAX's collectives and lax.ppermute only.
A program may use at most 128 MiB of HBM per device.

```python
import jax
import jax.numpy as jnp
from jax import lax

BASIS = 128
AUXF = 160
NEIGH = 4
RANGE = 3
GROUPS = 128
OFFSETS = 13


def draw_neighbours(key, part):
    base = jnp.arange(2 * RANGE, dtype=jnp.int32)
    shifts = jnp.where(base < RANGE, base - RANGE, base - RANGE + 1)
    scores = jax.random.randint(key, (GROUPS, 2 * RANGE), 0, 1 << 20, dtype=jnp.int32) * (2 * RANGE) + base[None, :]
    order = jnp.argsort(scores, axis=1, stable=True)
    picked = shifts[order[:, :NEIGH - 1]]
    full = jnp.concatenate([jnp.zeros((GROUPS, 1), jnp.int32), picked], axis=1)
    rows = jnp.arange(GROUPS, dtype=jnp.int32)[:, None]
    return jnp.mod(rows + full, GROUPS).astype(jnp.int32)


def plant(array, stream_key, smallest, high):
    dims = array.shape
    place = [jax.random.randint(jax.random.fold_in(stream_key, axis), (), 0, dims[axis]) for axis in range(len(dims))]
    array = array.at[tuple(place)].set(smallest)
    longest = dims.index(max(dims))
    place[longest] = (place[longest] + 1) % dims[longest]
    return array.at[tuple(place)].set(high)


def steps_of(rng, dims, pieces, least, high):
    def one(axis_at, parts):
        steps = jax.random.uniform(jax.random.fold_in(jax.random.fold_in(rng, 6), axis_at), (parts,), jnp.float32, least / len(pieces), high / len(pieces))
        return jnp.repeat(jnp.exp(steps), dims[axis_at] // parts).reshape((-1,) + (1,) * (len(dims) - axis_at - 1))

    gain = one(*pieces[0])
    for cut in pieces[1:]:
        gain = gain * one(*cut)
    return gain


def scatter_about(stream_key, extent, scale, limit, cuts=(), held_as=jnp.bfloat16):
    values = scale * jax.random.normal(stream_key, extent, jnp.float32)
    if cuts:
        values = values * steps_of(stream_key, extent, cuts, -0.22, 0.18)
    return jnp.clip(values, -limit, limit).astype(held_as)


def setup_inputs(seed: int = 0) -> dict:
    arg_keys = jax.random.split(jax.random.key(seed), 6)
    three_index = scatter_about(arg_keys[0], (GROUPS, NEIGH, AUXF, BASIS, BASIS), 0.025, 0.14941406, ((0, 64), (2, 4)))
    density = scatter_about(arg_keys[1], (GROUPS, OFFSETS, BASIS, BASIS), 1.0, 6.0, ((0, 64),))
    neighbours = draw_neighbours(jax.random.fold_in(arg_keys[5], 71), 0)
    partner = plant(jax.random.randint(arg_keys[3], (GROUPS, NEIGH), 0, NEIGH), jax.random.fold_in(arg_keys[3], 1), 0, NEIGH - 1).astype(jnp.int32)
    block_mask = plant((jax.random.randint(arg_keys[4], (GROUPS, NEIGH), 0, 4) < 3).astype(jnp.int32), jax.random.fold_in(arg_keys[4], 1), 0, 1)
    return {"three_index": three_index, "density": density, "neighbours": neighbours, "partner": partner, "block_mask": block_mask}


def reference(three_index, density, neighbours, partner, block_mask):
    center = 2 * RANGE

    def visit(band, group):
        blocks = three_index[group].astype(jnp.float32)
        near = neighbours[group]
        pick = partner[group]
        masks = block_mask[group]
        weight = (masks * masks[pick]).astype(jnp.float32)
        other = near[pick]
        offset = jnp.mod(other - near + center, GROUPS).astype(jnp.int32)
        far = density[near, offset].astype(jnp.float32)
        paired = blocks[pick]
        left = jnp.einsum("jac,jpmc->jpam", far, paired)
        left = lax.optimization_barrier(left.astype(jnp.bfloat16)).astype(jnp.float32)
        own = jnp.einsum("jpma,jpan->jmn", blocks, left)
        own = jnp.sum(own * weight[:, None, None], axis=0)
        home = density[group, center].astype(jnp.float32)
        right = jnp.einsum("ml,jplc->jpmc", home, paired)
        right = lax.optimization_barrier(right.astype(jnp.bfloat16)).astype(jnp.float32)
        cross = jnp.einsum("jpmn,jpmc->jnc", blocks, right) * weight[:, None, None]
        band = band.at[group, center].add(own)
        band = band.at[near, offset].add(cross)
        return band, None

    start = jnp.zeros((GROUPS, 4 * RANGE + 1, BASIS, BASIS), jnp.float32)
    band, unused = lax.scan(visit, start, jnp.arange(GROUPS, dtype=jnp.int32))
    return band
```

```python
import jax
import jax.numpy as jnp
from jax import lax
from jax.experimental import pallas as pl
from jax.experimental.pallas import tpu as pltpu
from jax.sharding import PartitionSpec as P

BASIS = 128
SLAB = 8
ROWS = 32
EDGE = 16
f32 = jnp.float32
bf16 = jnp.bfloat16
VM = pl.BlockSpec(memory_space=pltpu.VMEM)
SM = pl.BlockSpec(memory_space=pltpu.SMEM)
ANY = pl.BlockSpec(memory_space=pl.ANY)


def swapped(value, kind):
    count = lax.axis_size("sfc")
    if kind == "a":
        step, first = 1, [0]
        period = 2
    elif kind == "b":
        step, first = 1, [1]
        period = 2
    elif kind == "c":
        step, first = 2, [0, 1]
        period = 4
    else:
        step, first = 2, [2, 3]
        period = 4
    pairs = []
    for base in range(0, count, period):
        for start in first:
            low = (base + start) % count
            high = (base + start + step) % count
            pairs += [(low, high), (high, low)]
    return lax.ppermute(value, "sfc", pairs)


def side_by_side(parts):
    return jnp.concatenate(parts, axis=1)


def stacked(wide, parts):
    return jnp.concatenate([wide[:, BASIS * i : BASIS * (i + 1)] for i in range(parts)], axis=0)


def right_cross(home, paired, block, held):
    aux = paired.shape[0]
    for p in range(0, aux, SLAB):
        wide = side_by_side([paired[p + i] for i in range(SLAB)])
        right = jnp.dot(home, wide, preferred_element_type=f32).astype(bf16)
        held[pl.ds(p * BASIS, SLAB * BASIS)] = stacked(right, SLAB)
    flat = block[...].reshape(aux * BASIS, BASIS)
    return lax.dot_general(flat, held[...], (((0,), (0,)), ((), ())), preferred_element_type=f32)


def left_own(far, paired, block, held):
    aux = paired.shape[0]
    for p in range(0, aux, SLAB):
        tall = paired[pl.ds(p, SLAB)].reshape(SLAB * BASIS, BASIS)
        left = lax.dot_general(
            far, tall, (((1,), (1,)), ((), ())), preferred_element_type=f32
        ).astype(bf16)
        held[pl.ds(p * BASIS, SLAB * BASIS)] = stacked(left, SLAB)
    wide = side_by_side([block[p] for p in range(aux)])
    return jnp.dot(wide, held[...], preferred_element_type=f32)


def geometry(near, pick, mask, mine, total, g, j):
    k = pick[g, j]
    shift = lax.rem(near[g, j] - 2 * mine - g + total + 64, total) - 64
    offset = lax.rem(near[g, k] - near[g, j] + 6 + total, total)
    active = mask[g, j] * mask[g, k]
    return k, shift, offset, active


def pack_kernel(where, density, out_a, out_b, out_c, out_d, sems):
    mine = where[0]
    plus_a = 1 - lax.rem(mine, 2)
    plus_c = 1 - lax.rem(mine, 4) // 2
    copies = []
    for ref, plus in ((out_b, 1 - plus_a), (out_a, plus_a)):
        copies.append((density.at[0, pl.ds(1 + 4 * plus, 8)], ref.at[pl.ds(0, 8)]))
        copies.append((density.at[1, pl.ds(4 * plus, 8)], ref.at[pl.ds(8, 8)]))
    for ref, plus in ((out_d, 1 - plus_c), (out_c, plus_c)):
        copies.append((density.at[plus, pl.ds(6 * plus, 7)], ref))
    made = [pltpu.make_async_copy(s, d, sems.at[i]) for i, (s, d) in enumerate(copies)]
    for copy in made:
        copy.start()
    for copy in made:
        copy.wait()


def cross_kernel(
    where, near, pick, mask, blocks, density, out_a, out_b, out_c, out_d, out_l, own, held
):
    mine = where[0]
    total = where[1]
    odd = lax.rem(mine, 2)
    upper = lax.rem(mine, 4) // 2
    for ref in (out_a, out_b, out_c, out_d, out_l):
        ref[...] = jnp.zeros_like(ref)
    own[...] = jnp.zeros_like(own)

    def visit(i, carry):
        g = i // 4
        j = lax.rem(i, 4)
        k, shift, offset, active = geometry(near, pick, mask, mine, total, g, j)
        place = g + shift
        reach = (place + 4) // 2 - 2
        within = place - 2 * reach
        label = (within * 13 + offset).astype(f32)

        @pl.when(active != 0)
        def _():
            value = right_cross(density[g, 6], blocks.at[g, k], blocks.at[g, j], held)
            value = value.astype(bf16)
            tag = jnp.full((EDGE, BASIS), label, f32).astype(bf16)

            def put(ref, slot):
                ref[slot, pl.ds(0, BASIS)] = value
                ref[slot, pl.ds(BASIS, EDGE)] = tag

            ahead = jnp.where(reach > 0, 1, 0)
            slot = jnp.where(reach > 0, 3 * g + shift - 2, g - shift - 1)
            slot = jnp.clip(slot, 0, 3)
            one = jnp.abs(reach) == 1
            two = jnp.abs(reach) == 2

            @pl.when(reach == 0)
            def _():
                put(out_l, jnp.clip(3 * g + shift, 0, 3))

            @pl.when(jnp.logical_and(one, ahead != odd))
            def _():
                put(out_a, slot)

            @pl.when(jnp.logical_and(one, ahead == odd))
            def _():
                put(out_b, slot)

            @pl.when(jnp.logical_and(two, ahead != upper))
            def _():
                put(out_c, 0)

            @pl.when(jnp.logical_and(two, ahead == upper))
            def _():
                put(out_d, 0)

        @pl.when(jnp.logical_and(active != 0, reach == 0))
        def _():
            far = density[within, offset]
            own[g] += left_own(far, blocks.at[g, k], blocks.at[g, j], held)

        return carry

    lax.fori_loop(0, 8, visit, 0)


def own_kernel(
    where, near, pick, mask, blocks, far_a, far_b, far_c, far_d, own_in, own, held, far
):
    mine = where[0]
    total = where[1]
    odd = lax.rem(mine, 2)
    upper = lax.rem(mine, 4) // 2
    own[...] = own_in[...]

    def visit(i, carry):
        g = i // 4
        j = lax.rem(i, 4)
        k, shift, offset, active = geometry(near, pick, mask, mine, total, g, j)
        place = g + shift
        reach = (place + 4) // 2 - 2
        within = place - 2 * reach
        ahead = jnp.where(reach > 0, 1, 0)

        @pl.when(jnp.logical_and(active != 0, reach != 0))
        def _():
            start = jnp.where(reach > 0, 1 - within, 5 - within)
            index = jnp.clip(within * 8 + offset - start, 0, 15)
            single = jnp.clip(offset - 6 * (1 - ahead), 0, 6)
            one = jnp.abs(reach) == 1
            two = jnp.abs(reach) == 2

            @pl.when(jnp.logical_and(one, ahead != odd))
            def _():
                far[...] = far_a[index]

            @pl.when(jnp.logical_and(one, ahead == odd))
            def _():
                far[...] = far_b[index]

            @pl.when(jnp.logical_and(two, ahead != upper))
            def _():
                far[...] = far_c[single]

            @pl.when(jnp.logical_and(two, ahead == upper))
            def _():
                far[...] = far_d[single]

            own[g] += left_own(far[...], blocks.at[g, k], blocks.at[g, j], held)

        return carry

    lax.fori_loop(0, 8, visit, 0)


def rows_kernel(where, in_a, in_b, in_c, in_d, in_l, own, *outs):
    side = where[2]
    for step, out in enumerate(outs):
        start = pl.multiple_of(lax.rem(side + step + 1, 4) * ROWS, ROWS)
        at = 0
        for ref in (in_a, in_b, in_c, in_d, in_l):
            for slot in range(ref.shape[0]):
                out[at] = ref[slot, pl.ds(start, ROWS)]
                at += 1
        for g in range(2):
            out[at] = own[g, pl.ds(start, ROWS)].astype(bf16)
            at += 1


def band_kernel(where, in_a, in_b, in_c, in_d, in_l, own, from_1, from_2, from_3, band):
    side = where[2]
    start = pl.multiple_of(side * ROWS, ROWS)
    band[...] = jnp.zeros_like(band)

    def others(at):
        return (
            from_1[at].astype(f32) + from_2[at].astype(f32) + from_3[at].astype(f32)
        )

    at = 0
    found = []
    for ref in (in_a, in_b, in_c, in_d, in_l):
        for slot in range(ref.shape[0]):
            label = jnp.max(ref[slot, pl.ds(BASIS, EDGE)].astype(f32)).astype(jnp.int32)
            value = ref[slot, pl.ds(start, ROWS)].astype(f32) + others(at)
            found.append((jnp.clip(label, 0, 25), value))
            at += 1
    for g in range(2):
        found.append((13 * g + 6, own[g, pl.ds(start, ROWS)] + others(at)))
        at += 1
    for label, value in found:
        band[label] += value


def local(three_index, density, neighbours, partner, block_mask):
    total = 2 * lax.axis_size("sfc")
    where = jnp.stack(
        [lax.axis_index("sfc"), jnp.int32(total), lax.axis_index("aux")]
    ).astype(jnp.int32)
    ints = (where, neighbours, partner, block_mask)
    limit = pltpu.CompilerParams(vmem_limit_bytes=24 << 20)

    def shape(*dims, dtype=bf16):
        return jax.ShapeDtypeStruct(dims, dtype)

    packed = pl.pallas_call(
        pack_kernel,
        in_specs=[SM, ANY],
        out_specs=[ANY] * 4,
        out_shape=[shape(16, 128, 128), shape(16, 128, 128), shape(7, 128, 128), shape(7, 128, 128)],
        scratch_shapes=[pltpu.SemaphoreType.DMA((6,))],
        name="pack",
    )(where, density)
    far_b = swapped(packed[1], "b")
    far_d = swapped(packed[3], "d")
    far_a = swapped(packed[0], "a")
    far_c = swapped(packed[2], "c")

    tall = BASIS + EDGE
    crosses = pl.pallas_call(
        cross_kernel,
        in_specs=[SM] * 4 + [VM, VM],
        out_specs=[VM] * 6,
        out_shape=[
            shape(4, tall, 128),
            shape(4, tall, 128),
            shape(1, tall, 128),
            shape(1, tall, 128),
            shape(4, tall, 128),
            shape(2, 128, 128, dtype=f32),
        ],
        scratch_shapes=[pltpu.VMEM((40 * BASIS, BASIS), bf16)],
        compiler_params=limit,
        name="cross",
    )(*ints, three_index, density)
    out_a, out_b, out_c, out_d, in_l, own_near = crosses
    in_b = swapped(out_b, "b")
    in_d = swapped(out_d, "d")
    in_a = swapped(out_a, "a")
    in_c = swapped(out_c, "c")

    own = pl.pallas_call(
        own_kernel,
        in_specs=[SM] * 4 + [VM] * 6,
        out_specs=VM,
        out_shape=shape(2, 128, 128, dtype=f32),
        scratch_shapes=[pltpu.VMEM((40 * BASIS, BASIS), bf16), pltpu.VMEM((128, 128), bf16)],
        compiler_params=limit,
        name="own",
    )(*ints, three_index, far_a, far_b, far_c, far_d, own_near)

    arrived = (in_a, in_b, in_c, in_d, in_l, own)
    sends = pl.pallas_call(
        rows_kernel,
        in_specs=[SM] + [VM] * 6,
        out_specs=[VM] * 3,
        out_shape=[shape(16, ROWS, 128)] * 3,
        name="rows",
    )(where, *arrived)
    received = []
    for step, send in enumerate(sends):
        pairs = [(x, (x + step + 1) % 4) for x in range(4)]
        received.append(lax.ppermute(send, "aux", pairs))
    band = pl.pallas_call(
        band_kernel,
        in_specs=[SM] + [VM] * 9,
        out_specs=VM,
        out_shape=shape(26, ROWS, 128, dtype=f32),
        name="band",
    )(where, *arrived, *received)
    return band.reshape(2, 13, ROWS, 128)


def solution(mesh):
    return jax.shard_map(
        local,
        mesh=mesh,
        in_specs=(
            P("sfc", None, "aux", None, None),
            P("sfc", None, None, None),
            P("sfc", None),
            P("sfc", None),
            P("sfc", None),
        ),
        out_specs=P("sfc", None, "aux", None),
        check_vma=False,
    )
```

```python
import jax
import jax.numpy as jnp
from jax import lax
from jax.experimental import pallas as pl
from jax.experimental.pallas import tpu as pltpu
from jax.sharding import PartitionSpec as P

BASIS = 128
SLAB = 8
ROWS = 32
EDGE = 16
f32 = jnp.float32
bf16 = jnp.bfloat16
VM = pl.BlockSpec(memory_space=pltpu.VMEM)
SM = pl.BlockSpec(memory_space=pltpu.SMEM)
ANY = pl.BlockSpec(memory_space=pl.ANY)


def swapped(value, kind):
    count = lax.axis_size("sfc")
    if kind == "a":
        step, first = 1, [0]
        period = 2
    elif kind == "b":
        step, first = 1, [1]
        period = 2
    elif kind == "c":
        step, first = 2, [0, 1]
        period = 4
    else:
        step, first = 2, [2, 3]
        period = 4
    pairs = []
    for base in range(0, count, period):
        for start in first:
            low = (base + start) % count
            high = (base + start + step) % count
            pairs += [(low, high), (high, low)]
    return lax.ppermute(value, "sfc", pairs)


def side_by_side(parts):
    return jnp.concatenate(parts, axis=1)


def stacked(wide, parts):
    return jnp.concatenate([wide[:, BASIS * i : BASIS * (i + 1)] for i in range(parts)], axis=0)


def right_cross(home, paired, block, held):
    aux = paired.shape[0]
    for p in range(0, aux, SLAB):
        wide = side_by_side([paired[p + i] for i in range(SLAB)])
        right = jnp.dot(home, wide, preferred_element_type=f32).astype(bf16)
        held[pl.ds(p * BASIS, SLAB * BASIS)] = stacked(right, SLAB)
    flat = block[...].reshape(aux * BASIS, BASIS)
    return lax.dot_general(flat, held[...], (((0,), (0,)), ((), ())), preferred_element_type=f32)


def left_own(far, paired, block, held):
    aux = paired.shape[0]
    for p in range(0, aux, SLAB):
        tall = paired[pl.ds(p, SLAB)].reshape(SLAB * BASIS, BASIS)
        left = lax.dot_general(
            far, tall, (((1,), (1,)), ((), ())), preferred_element_type=f32
        ).astype(bf16)
        held[pl.ds(p * BASIS, SLAB * BASIS)] = stacked(left, SLAB)
    wide = side_by_side([block[p] for p in range(aux)])
    return jnp.dot(wide, held[...], preferred_element_type=f32)


def fetch_ints(sources, targets, sems):
    copies = [pltpu.make_async_copy(s, t, sems.at[i]) for i, (s, t) in enumerate(zip(sources, targets))]
    for copy in copies:
        copy.start()
    for copy in copies:
        copy.wait()


class Pair:
    def __init__(self, i, near, pick, mask):
        mine = lax.axis_index("sfc")
        total = 2 * lax.axis_size("sfc")
        self.g = g = i // 4
        self.j = j = lax.rem(i, 4)
        self.k = k = pick[g, j]
        self.shift = lax.rem(near[g, j] - 2 * mine - g + total + 64, total) - 64
        self.offset = lax.rem(near[g, k] - near[g, j] + 6 + total, total)
        self.active = mask[g, j] * mask[g, k] != 0
        place = g + self.shift
        self.reach = (place + 4) // 2 - 2
        self.within = place - 2 * self.reach
        self.ahead = jnp.where(self.reach > 0, 1, 0)
        one = jnp.abs(self.reach) == 1
        two = jnp.abs(self.reach) == 2
        odd = lax.rem(mine, 2)
        upper = lax.rem(mine, 4) // 2
        self.in_a = jnp.logical_and(one, self.ahead != odd)
        self.in_b = jnp.logical_and(one, self.ahead == odd)
        self.in_c = jnp.logical_and(two, self.ahead != upper)
        self.in_d = jnp.logical_and(two, self.ahead == upper)
        self.one = one
        self.two = two

    def when(self, condition):
        return pl.when(jnp.logical_and(self.active, condition))


def pack_kernel(density, out_b, out_d, out_a, out_c, sems):
    mine = lax.axis_index("sfc")
    plus_a = 1 - lax.rem(mine, 2)
    plus_c = 1 - lax.rem(mine, 4) // 2
    copies = []
    for ref, plus in ((out_b, 1 - plus_a), (out_a, plus_a)):
        copies.append((density.at[0, pl.ds(1 + 4 * plus, 8)], ref.at[pl.ds(0, 8)]))
        copies.append((density.at[1, pl.ds(4 * plus, 8)], ref.at[pl.ds(8, 8)]))
    for ref, plus in ((out_d, 1 - plus_c), (out_c, plus_c)):
        copies.append((density.at[plus, pl.ds(6 * plus, 7)], ref))
    made = [pltpu.make_async_copy(s, d, sems.at[i]) for i, (s, d) in enumerate(copies)]
    for copy in made:
        copy.start()
    for copy in made:
        copy.wait()


def put(ref, slot, value, pair):
    label = (pair.within * 13 + pair.offset).astype(f32)
    ref[slot, pl.ds(0, BASIS)] = value
    ref[slot, pl.ds(BASIS, EDGE)] = jnp.full((EDGE, BASIS), label, f32).astype(bf16)


def cross_kernel(
    near_in, pick_in, mask_in, source, density,
    out_b, out_d, out_a, out_c, inside, blocks,
    near, pick, mask, home, held, int_sems, home_sem, sems,
):
    def loads(g):
        return [
            pltpu.make_async_copy(source.at[g, j], blocks.at[g, j], sems.at[g, j])
            for j in range(4)
        ]

    center = pltpu.make_async_copy(density.at[:, 6], home, home_sem)
    center.start()
    for copy in loads(0):
        copy.start()
    fetch_ints((near_in, pick_in, mask_in), (near, pick, mask), int_sems)
    for ref in (out_b, out_d, out_a, out_c, inside):
        ref[...] = jnp.zeros_like(ref)
    center.wait()

    def visit(i, carry):
        pair = Pair(i, near, pick, mask)
        g, j, k, shift = pair.g, pair.j, pair.k, pair.shift

        @pl.when(pair.active)
        def _():
            value = right_cross(home[g], blocks.at[g, k], blocks.at[g, j], held).astype(bf16)
            slot = jnp.where(pair.reach > 0, 3 * g + shift - 2, g - shift - 1)
            slot = jnp.clip(slot, 0, 3)

            @pl.when(pair.reach == 0)
            def _():
                put(inside, jnp.clip(3 * g + shift, 0, 3), value, pair)

            @pl.when(pair.in_a)
            def _():
                put(out_a, slot, value, pair)

            @pl.when(pair.in_b)
            def _():
                put(out_b, slot, value, pair)

            @pl.when(pair.in_c)
            def _():
                put(out_c, 0, value, pair)

            @pl.when(pair.in_d)
            def _():
                put(out_d, 0, value, pair)

        return carry

    def group(g, carry):
        for j in range(4):
            pltpu.make_async_copy(source.at[0, 0], blocks.at[0, 0], sems.at[g, j]).wait()

        @pl.when(g == 0)
        def _():
            for copy in loads(1):
                copy.start()

        return lax.fori_loop(4 * g, 4 * g + 4, visit, carry)

    lax.fori_loop(0, 2, group, 0)


def own_kernel(
    far_b, far_d, far_a, far_c, near_in, pick_in, mask_in, blocks, density, own,
    near, pick, mask, held, far, whole, int_sems, whole_sem,
):
    copy = pltpu.make_async_copy(density, whole, whole_sem)
    copy.start()
    fetch_ints((near_in, pick_in, mask_in), (near, pick, mask), int_sems)
    own[...] = jnp.zeros_like(own)
    copy.wait()

    def visit(i, carry):
        pair = Pair(i, near, pick, mask)
        g, j, k = pair.g, pair.j, pair.k

        @pl.when(pair.active)
        def _():
            start = jnp.where(pair.reach > 0, 1 - pair.within, 5 - pair.within)
            index = jnp.clip(pair.within * 8 + pair.offset - start, 0, 15)
            single = jnp.clip(pair.offset - 6 * (1 - pair.ahead), 0, 6)

            @pl.when(pair.reach == 0)
            def _():
                far[...] = whole[pair.within, pair.offset]

            @pl.when(pair.in_a)
            def _():
                far[...] = far_a[index]

            @pl.when(pair.in_b)
            def _():
                far[...] = far_b[index]

            @pl.when(pair.in_c)
            def _():
                far[...] = far_c[single]

            @pl.when(pair.in_d)
            def _():
                far[...] = far_d[single]

            own[g] += left_own(far[...], blocks.at[g, k], blocks.at[g, j], held)

        return carry

    lax.fori_loop(0, 8, visit, 0)


def rows_kernel(in_b, in_d, in_a, in_c, in_l, own, *outs):
    side = lax.axis_index("aux")
    for step, out in enumerate(outs):
        start = pl.multiple_of(lax.rem(side + step + 1, 4) * ROWS, ROWS)
        at = 0
        for ref in (in_b, in_d, in_a, in_c, in_l):
            for slot in range(ref.shape[0]):
                out[at] = ref[slot, pl.ds(start, ROWS)]
                at += 1
        for g in range(2):
            out[at] = own[g, pl.ds(start, ROWS)].astype(bf16)
            at += 1


def band_kernel(in_b, in_d, in_a, in_c, in_l, own, from_1, from_2, from_3, band):
    side = lax.axis_index("aux")
    start = pl.multiple_of(side * ROWS, ROWS)
    band[...] = jnp.zeros_like(band)

    def others(at):
        return (
            from_1[at].astype(f32) + from_2[at].astype(f32) + from_3[at].astype(f32)
        )

    at = 0
    found = []
    for ref in (in_b, in_d, in_a, in_c, in_l):
        for slot in range(ref.shape[0]):
            label = jnp.max(ref[slot, pl.ds(BASIS, EDGE)].astype(f32)).astype(jnp.int32)
            value = ref[slot, pl.ds(start, ROWS)].astype(f32) + others(at)
            found.append((jnp.clip(label, 0, 25), value))
            at += 1
    for g in range(2):
        found.append((13 * g + 6, own[g, pl.ds(start, ROWS)] + others(at)))
        at += 1
    for label, value in found:
        band[label] += value


def shape(*dims, dtype=bf16):
    return jax.ShapeDtypeStruct(dims, dtype)


def int_scratch():
    return [pltpu.SMEM((2, 4), jnp.int32)] * 3


def local(three_index, density, neighbours, partner, block_mask):
    limit = pltpu.CompilerParams(vmem_limit_bytes=8 << 20)
    small = pltpu.CompilerParams(vmem_limit_bytes=4 << 20)
    three_index, density, neighbours, partner, block_mask = [
        pltpu.with_memory_space_constraint(x, pltpu.HBM)
        for x in (three_index, density, neighbours, partner, block_mask)
    ]
    ints = (neighbours, partner, block_mask)
    dma = pltpu.SemaphoreType.DMA
    packed = pl.pallas_call(
        pack_kernel,
        in_specs=[ANY],
        out_specs=[VM] * 4,
        out_shape=[shape(16, 128, 128), shape(7, 128, 128), shape(16, 128, 128), shape(7, 128, 128)],
        scratch_shapes=[dma((6,))],
        compiler_params=small,
        name="pack",
    )(density)
    far_b = swapped(packed[0], "b")
    far_d = swapped(packed[1], "d")
    far_a = swapped(packed[2], "a")
    far_c = swapped(packed[3], "c")

    tall = BASIS + EDGE
    held = pltpu.VMEM((40 * BASIS, BASIS), bf16)
    out_b, out_d, out_a, out_c, inside, blocks = pl.pallas_call(
        cross_kernel,
        in_specs=[ANY] * 5,
        out_specs=[VM] * 6,
        out_shape=[
            shape(4, tall, 128),
            shape(1, tall, 128),
            shape(4, tall, 128),
            shape(1, tall, 128),
            shape(4, tall, 128),
            pltpu.VMEM(three_index.shape, bf16),
        ],
        scratch_shapes=int_scratch()
        + [pltpu.VMEM((2, 128, 128), bf16), held]
        + [dma((3,)), dma(()), dma((2, 4))],
        compiler_params=limit,
        name="cross",
    )(*ints, three_index, density)
    in_b = swapped(out_b, "b")
    in_d = swapped(out_d, "d")
    in_a = swapped(out_a, "a")
    in_c = swapped(out_c, "c")

    own = pl.pallas_call(
        own_kernel,
        in_specs=[VM] * 4 + [ANY] * 3 + [VM, ANY],
        out_specs=VM,
        out_shape=shape(2, 128, 128, dtype=f32),
        scratch_shapes=int_scratch()
        + [held, pltpu.VMEM((128, 128), bf16), pltpu.VMEM(density.shape, bf16), dma((3,)), dma(())],
        compiler_params=limit,
        name="own",
    )(far_b, far_d, far_a, far_c, *ints, blocks, density)

    arrived = (in_b, in_d, in_a, in_c, inside, own)
    sends = pl.pallas_call(
        rows_kernel,
        in_specs=[VM] * 6,
        out_specs=[VM] * 3,
        out_shape=[shape(16, ROWS, 128)] * 3,
        compiler_params=small,
        name="rows",
    )(*arrived)
    received = []
    for step, send in enumerate(sends):
        pairs = [(x, (x + step + 1) % 4) for x in range(4)]
        received.append(lax.ppermute(send, "aux", pairs))
    band = pl.pallas_call(
        band_kernel,
        in_specs=[VM] * 9,
        out_specs=VM,
        out_shape=shape(26, ROWS, 128, dtype=f32),
        compiler_params=small,
        name="band",
    )(*arrived, *received)
    return band.reshape(2, 13, ROWS, 128)


def solution(mesh):
    return jax.shard_map(
        local,
        mesh=mesh,
        in_specs=(
            P("sfc", None, "aux", None, None),
            P("sfc", None, None, None),
            P("sfc", None),
            P("sfc", None),
            P("sfc", None),
        ),
        out_specs=P("sfc", None, "aux", None),
        check_vma=False,
    )
```

```python
import jax
import jax.numpy as jnp
from jax import lax
from jax.experimental import pallas as pl
from jax.experimental.pallas import tpu as pltpu
from jax.sharding import PartitionSpec as P

BASIS = 128
SLAB = 8
ROWS = 32
EDGE = 16
FLIGHT = 2
f32 = jnp.float32
bf16 = jnp.bfloat16
VM = pl.BlockSpec(memory_space=pltpu.VMEM)
SM = pl.BlockSpec(memory_space=pltpu.SMEM)
ANY = pl.BlockSpec(memory_space=pl.ANY)


def swapped(value, kind):
    count = lax.axis_size("sfc")
    if kind == "a":
        step, first = 1, [0]
        period = 2
    elif kind == "b":
        step, first = 1, [1]
        period = 2
    elif kind == "c":
        step, first = 2, [0, 1]
        period = 4
    else:
        step, first = 2, [2, 3]
        period = 4
    pairs = []
    for base in range(0, count, period):
        for start in first:
            low = (base + start) % count
            high = (base + start + step) % count
            pairs += [(low, high), (high, low)]
    return lax.ppermute(value, "sfc", pairs)


def side_by_side(parts):
    return jnp.concatenate(parts, axis=1)


def stacked(wide, parts):
    return jnp.concatenate([wide[:, BASIS * i : BASIS * (i + 1)] for i in range(parts)], axis=0)


def right_cross(home, paired, block, held):
    aux = paired.shape[0]
    for p in range(0, aux, SLAB):
        wide = side_by_side([paired[p + i] for i in range(SLAB)])
        right = jnp.dot(home, wide, preferred_element_type=f32).astype(bf16)
        held[pl.ds(p * BASIS, SLAB * BASIS)] = stacked(right, SLAB)
    flat = block[...].reshape(aux * BASIS, BASIS)
    return lax.dot_general(flat, held[...], (((0,), (0,)), ((), ())), preferred_element_type=f32)


def left_own(far, paired, block, held):
    aux = paired.shape[0]
    for p in range(0, aux, SLAB):
        tall = paired[pl.ds(p, SLAB)].reshape(SLAB * BASIS, BASIS)
        left = lax.dot_general(
            far, tall, (((1,), (1,)), ((), ())), preferred_element_type=f32
        ).astype(bf16)
        held[pl.ds(p * BASIS, SLAB * BASIS)] = stacked(left, SLAB)
    wide = side_by_side([block[p] for p in range(aux)])
    return jnp.dot(wide, held[...], preferred_element_type=f32)


def fetch_ints(sources, targets, sems):
    copies = [pltpu.make_async_copy(s, t, sems.at[i]) for i, (s, t) in enumerate(zip(sources, targets))]
    for copy in copies:
        copy.start()
    for copy in copies:
        copy.wait()


class Pair:
    def __init__(self, i, near, pick, mask):
        mine = lax.axis_index("sfc")
        total = 2 * lax.axis_size("sfc")
        self.g = g = i // 4
        self.j = j = lax.rem(i, 4)
        self.k = k = pick[g, j]
        self.shift = lax.rem(near[g, j] - 2 * mine - g + total + 64, total) - 64
        self.offset = lax.rem(near[g, k] - near[g, j] + 6 + total, total)
        self.active = mask[g, j] * mask[g, k] != 0
        place = g + self.shift
        self.reach = (place + 4) // 2 - 2
        self.within = place - 2 * self.reach
        self.ahead = jnp.where(self.reach > 0, 1, 0)
        one = jnp.abs(self.reach) == 1
        two = jnp.abs(self.reach) == 2
        odd = lax.rem(mine, 2)
        upper = lax.rem(mine, 4) // 2
        self.in_a = jnp.logical_and(one, self.ahead != odd)
        self.in_b = jnp.logical_and(one, self.ahead == odd)
        self.in_c = jnp.logical_and(two, self.ahead != upper)
        self.in_d = jnp.logical_and(two, self.ahead == upper)
        self.one = one
        self.two = two

    def when(self, condition):
        return pl.when(jnp.logical_and(self.active, condition))


def pack_kernel(
    density, near_in, pick_in, mask_in, out_b, out_d, out_a, out_c, near, pick, mask, sems
):
    mine = lax.axis_index("sfc")
    plus_a = 1 - lax.rem(mine, 2)
    plus_c = 1 - lax.rem(mine, 4) // 2
    copies = []
    for ref, plus in ((out_b, 1 - plus_a), (out_a, plus_a)):
        copies.append((density.at[0, pl.ds(1 + 4 * plus, 8)], ref.at[pl.ds(0, 8)]))
        copies.append((density.at[1, pl.ds(4 * plus, 8)], ref.at[pl.ds(8, 8)]))
    for ref, plus in ((out_d, 1 - plus_c), (out_c, plus_c)):
        copies.append((density.at[plus, pl.ds(6 * plus, 7)], ref))
    copies += [(near_in, near), (pick_in, pick), (mask_in, mask)]
    made = [pltpu.make_async_copy(s, d, sems.at[i]) for i, (s, d) in enumerate(copies)]
    for copy in made:
        copy.start()
    for copy in made:
        copy.wait()


def put(ref, slot, value, pair):
    label = (pair.within * 13 + pair.offset).astype(f32)
    ref[slot, pl.ds(0, BASIS)] = value
    ref[slot, pl.ds(BASIS, EDGE)] = jnp.full((EDGE, BASIS), label, f32).astype(bf16)


def cross_kernel(
    near_in, pick_in, mask_in, source, density,
    out_b, out_d, out_a, out_c, inside, blocks, whole,
    near, pick, mask, queue, state, upto, held, int_sems, whole_sem, sems,
):
    copy = pltpu.make_async_copy(density, whole, whole_sem)
    copy.start()
    fetch_ints((near_in, pick_in, mask_in), (near, pick, mask), int_sems)
    for i in range(8):
        state[i] = 0

    def demand(t, length):
        pair = Pair(t, near, pick, mask)
        for other in (pair.k, pair.j):
            index = 4 * pair.g + other
            fresh = jnp.logical_and(state[index] == 0, pair.active)

            @pl.when(fresh)
            def _():
                queue[length] = index
                state[index] = 1

            length = length + jnp.where(fresh, 1, 0)
        upto[t] = length
        return length

    length = lax.fori_loop(0, 8, demand, 0)

    def load(q, carry):
        @pl.when(q < length)
        def _():
            index = queue[q]
            g, j = index // 4, lax.rem(index, 4)
            pltpu.make_async_copy(source.at[g, j], blocks.at[g, j], sems.at[index]).start()

        return carry

    def arrive(q, carry):
        pltpu.make_async_copy(source.at[0, 0], blocks.at[0, 0], sems.at[queue[q]]).wait()
        return load(q + FLIGHT, carry)

    lax.fori_loop(0, FLIGHT, load, 0)
    for ref in (out_b, out_d, out_a, out_c, inside):
        ref[...] = jnp.zeros_like(ref)
    copy.wait()

    def store(pair, value):
        value = value.astype(bf16)
        g, shift = pair.g, pair.shift
        slot = jnp.where(pair.reach > 0, 3 * g + shift - 2, g - shift - 1)
        slot = jnp.clip(slot, 0, 3)

        @pl.when(pair.reach == 0)
        def _():
            put(inside, jnp.clip(3 * g + shift, 0, 3), value, pair)

        @pl.when(pair.in_a)
        def _():
            put(out_a, slot, value, pair)

        @pl.when(pair.in_b)
        def _():
            put(out_b, slot, value, pair)

        @pl.when(pair.in_c)
        def _():
            put(out_c, 0, value, pair)

        @pl.when(pair.in_d)
        def _():
            put(out_d, 0, value, pair)

    def visit(i, arrived):
        pair = Pair(i, near, pick, mask)
        g, j, k = pair.g, pair.j, pair.k
        lax.fori_loop(arrived, upto[i], arrive, 0)

        @pl.when(pair.active)
        def _():
            store(pair, right_cross(whole[g, 6], blocks.at[g, k], blocks.at[g, j], held))

        return upto[i]

    lax.fori_loop(0, 8, visit, 0)


def own_kernel(
    far_b, far_d, far_a, far_c, near_in, pick_in, mask_in, blocks, whole, own,
    near, pick, mask, held, far, int_sems,
):
    fetch_ints((near_in, pick_in, mask_in), (near, pick, mask), int_sems)
    own[...] = jnp.zeros_like(own)

    def visit(i, carry):
        pair = Pair(i, near, pick, mask)
        g, j, k = pair.g, pair.j, pair.k

        @pl.when(pair.active)
        def _():
            start = jnp.where(pair.reach > 0, 1 - pair.within, 5 - pair.within)
            index = jnp.clip(pair.within * 8 + pair.offset - start, 0, 15)
            single = jnp.clip(pair.offset - 6 * (1 - pair.ahead), 0, 6)

            @pl.when(pair.reach == 0)
            def _():
                far[...] = whole[pair.within, pair.offset]

            @pl.when(pair.in_a)
            def _():
                far[...] = far_a[index]

            @pl.when(pair.in_b)
            def _():
                far[...] = far_b[index]

            @pl.when(pair.in_c)
            def _():
                far[...] = far_c[single]

            @pl.when(pair.in_d)
            def _():
                far[...] = far_d[single]

            own[g] += left_own(far[...], blocks.at[g, k], blocks.at[g, j], held)

        return carry

    lax.fori_loop(0, 8, visit, 0)


def rows_kernel(in_d, in_b, in_a, in_c, in_l, own, *outs):
    side = lax.axis_index("aux")
    for step, out in enumerate(outs):
        start = pl.multiple_of(lax.rem(side + step + 1, 4) * ROWS, ROWS)
        at = 0
        for ref in (in_b, in_d, in_a, in_c, in_l):
            for slot in range(1 if ref is in_c or ref is in_d else 4):
                out[at] = ref[slot, pl.ds(start, ROWS)]
                at += 1
        for g in range(2):
            out[at] = own[g, pl.ds(start, ROWS)].astype(bf16)
            at += 1


def band_kernel(in_d, in_b, in_a, in_c, in_l, own, from_1, from_2, from_3, band):
    side = lax.axis_index("aux")
    start = pl.multiple_of(side * ROWS, ROWS)
    band[...] = jnp.zeros_like(band)

    def others(at):
        return (
            from_1[at].astype(f32) + from_2[at].astype(f32) + from_3[at].astype(f32)
        )

    at = 0
    found = []
    for ref in (in_b, in_d, in_a, in_c, in_l):
        for slot in range(1 if ref is in_c or ref is in_d else 4):
            label = jnp.max(ref[slot, pl.ds(BASIS, EDGE)].astype(f32)).astype(jnp.int32)
            value = ref[slot, pl.ds(start, ROWS)].astype(f32) + others(at)
            found.append((jnp.clip(label, 0, 25), value))
            at += 1
    for g in range(2):
        found.append((13 * g + 6, own[g, pl.ds(start, ROWS)] + others(at)))
        at += 1
    for label, value in found:
        band[label] += value


def shape(*dims, dtype=bf16):
    return jax.ShapeDtypeStruct(dims, dtype)


def int_scratch():
    return [pltpu.SMEM((2, 4), jnp.int32)] * 3


def local(three_index, density, neighbours, partner, block_mask):
    limit = pltpu.CompilerParams(vmem_limit_bytes=8 << 20)
    small = pltpu.CompilerParams(vmem_limit_bytes=4 << 20)
    three_index, density, neighbours, partner, block_mask = [
        pltpu.with_memory_space_constraint(x, pltpu.HBM)
        for x in (three_index, density, neighbours, partner, block_mask)
    ]
    ints = (neighbours, partner, block_mask)
    dma = pltpu.SemaphoreType.DMA
    packed = pl.pallas_call(
        pack_kernel,
        in_specs=[ANY] * 4,
        out_specs=[VM] * 7,
        out_shape=[shape(n, 128, 128) for n in (16, 7, 16, 7)]
        + [pltpu.VMEM((2, 4), jnp.int32)] * 3,
        scratch_shapes=[dma((9,))],
        compiler_params=small,
        name="pack",
    )(density, *ints)
    ints = packed[4:]
    far_b = swapped(packed[0], "b")
    far_d = swapped(packed[1], "d")
    far_a = swapped(packed[2], "a")
    far_c = swapped(packed[3], "c")

    tall = BASIS + EDGE
    held = pltpu.VMEM((40 * BASIS, BASIS), bf16)
    out_b, out_d, out_a, out_c, inside, blocks, whole = pl.pallas_call(
        cross_kernel,
        in_specs=[ANY] * 5,
        out_specs=[VM] * 7,
        out_shape=[
            shape(4, tall, 128),
            shape(4, tall, 128),
            shape(4, tall, 128),
            shape(4, tall, 128),
            shape(4, tall, 128),
            pltpu.VMEM(three_index.shape, bf16),
            pltpu.VMEM(density.shape, bf16),
        ],
        scratch_shapes=int_scratch()
        + [pltpu.SMEM((8,), jnp.int32)] * 3
        + [held, dma((3,)), dma(()), dma((8,))],
        compiler_params=limit,
        name="cross",
    )(*ints, three_index, density)
    in_b = swapped(out_b, "b")
    in_d = swapped(out_d, "d")
    in_a = swapped(out_a, "a")
    in_c = swapped(out_c, "c")

    own = pl.pallas_call(
        own_kernel,
        in_specs=[VM] * 4 + [ANY] * 3 + [VM, VM],
        out_specs=VM,
        out_shape=shape(2, 128, 128, dtype=f32),
        scratch_shapes=int_scratch() + [held, pltpu.VMEM((128, 128), bf16), dma((3,))],
        compiler_params=limit,
        name="own",
    )(far_b, far_d, far_a, far_c, *ints, blocks, whole)

    arrived = (in_d, in_b, in_a, in_c, inside, own)
    sends = pl.pallas_call(
        rows_kernel,
        in_specs=[VM] * 6,
        out_specs=[VM] * 3,
        out_shape=[shape(16, ROWS, 128)] * 3,
        compiler_params=small,
        name="rows",
    )(*arrived)
    received = []
    for step, send in enumerate(sends):
        pairs = [(x, (x + step + 1) % 4) for x in range(4)]
        received.append(lax.ppermute(send, "aux", pairs))
    band = pl.pallas_call(
        band_kernel,
        in_specs=[VM] * 9,
        out_specs=VM,
        out_shape=shape(26, ROWS, 128, dtype=f32),
        compiler_params=small,
        name="band",
    )(*arrived, *received)
    return band.reshape(2, 13, ROWS, 128)


def solution(mesh):
    return jax.shard_map(
        local,
        mesh=mesh,
        in_specs=(
            P("sfc", None, "aux", None, None),
            P("sfc", None, None, None),
            P("sfc", None),
            P("sfc", None),
            P("sfc", None),
        ),
        out_specs=P("sfc", None, "aux", None),
        check_vma=False,
    )
```

```python
import jax
import jax.numpy as jnp
from jax import lax
from jax.experimental import pallas as pl
from jax.experimental.pallas import tpu as pltpu
from jax.sharding import PartitionSpec as P

BASIS = 128
SLAB = 8
ROWS = 32
EDGE = 16
FLIGHT = 8
f32 = jnp.float32
bf16 = jnp.bfloat16
VM = pl.BlockSpec(memory_space=pltpu.VMEM)
SM = pl.BlockSpec(memory_space=pltpu.SMEM)
ANY = pl.BlockSpec(memory_space=pl.ANY)


def swapped(value, kind):
    count = lax.axis_size("sfc")
    if kind == "a":
        step, first = 1, [0]
        period = 2
    elif kind == "b":
        step, first = 1, [1]
        period = 2
    elif kind == "c":
        step, first = 2, [0, 1]
        period = 4
    else:
        step, first = 2, [2, 3]
        period = 4
    pairs = []
    for base in range(0, count, period):
        for start in first:
            low = (base + start) % count
            high = (base + start + step) % count
            pairs += [(low, high), (high, low)]
    return lax.ppermute(value, "sfc", pairs)


def side_by_side(parts):
    return jnp.concatenate(parts, axis=1)


def stacked(wide, parts):
    return jnp.concatenate([wide[:, BASIS * i : BASIS * (i + 1)] for i in range(parts)], axis=0)


def right_cross(home, paired, block, held):
    aux = paired.shape[0]
    for p in range(0, aux, SLAB):
        wide = side_by_side([paired[p + i] for i in range(SLAB)])
        right = jnp.dot(home, wide, preferred_element_type=f32).astype(bf16)
        held[pl.ds(p * BASIS, SLAB * BASIS)] = stacked(right, SLAB)
    flat = block[...].reshape(aux * BASIS, BASIS)
    return lax.dot_general(flat, held[...], (((0,), (0,)), ((), ())), preferred_element_type=f32)


def left_own(far, paired, block, held):
    aux = paired.shape[0]
    for p in range(0, aux, SLAB):
        tall = paired[pl.ds(p, SLAB)].reshape(SLAB * BASIS, BASIS)
        left = lax.dot_general(
            far, tall, (((1,), (1,)), ((), ())), preferred_element_type=f32
        ).astype(bf16)
        held[pl.ds(p * BASIS, SLAB * BASIS)] = stacked(left, SLAB)
    wide = side_by_side([block[p] for p in range(aux)])
    return jnp.dot(wide, held[...], preferred_element_type=f32)


def fetch_ints(sources, targets, sems):
    copies = [pltpu.make_async_copy(s, t, sems.at[i]) for i, (s, t) in enumerate(zip(sources, targets))]
    for copy in copies:
        copy.start()
    for copy in copies:
        copy.wait()


class Pair:
    def __init__(self, i, near, pick, mask):
        mine = lax.axis_index("sfc")
        total = 2 * lax.axis_size("sfc")
        self.g = g = i // 4
        self.j = j = lax.rem(i, 4)
        self.k = k = pick[g, j]
        self.shift = lax.rem(near[g, j] - 2 * mine - g + total + 64, total) - 64
        self.offset = lax.rem(near[g, k] - near[g, j] + 6 + total, total)
        self.active = mask[g, j] * mask[g, k] != 0
        place = g + self.shift
        self.reach = (place + 4) // 2 - 2
        self.within = place - 2 * self.reach
        self.ahead = jnp.where(self.reach > 0, 1, 0)
        one = jnp.abs(self.reach) == 1
        two = jnp.abs(self.reach) == 2
        odd = lax.rem(mine, 2)
        upper = lax.rem(mine, 4) // 2
        self.in_a = jnp.logical_and(one, self.ahead != odd)
        self.in_b = jnp.logical_and(one, self.ahead == odd)
        self.in_c = jnp.logical_and(two, self.ahead != upper)
        self.in_d = jnp.logical_and(two, self.ahead == upper)
        self.one = one
        self.two = two

    def when(self, condition):
        return pl.when(jnp.logical_and(self.active, condition))


def pack_kernel(
    density, near_in, pick_in, mask_in, out_b, out_d, out_a, out_c, near, pick, mask, sems
):
    mine = lax.axis_index("sfc")
    plus_a = 1 - lax.rem(mine, 2)
    plus_c = 1 - lax.rem(mine, 4) // 2
    copies = []
    for ref, plus in ((out_b, 1 - plus_a), (out_a, plus_a)):
        copies.append((density.at[0, pl.ds(1 + 4 * plus, 8)], ref.at[pl.ds(0, 8)]))
        copies.append((density.at[1, pl.ds(4 * plus, 8)], ref.at[pl.ds(8, 8)]))
    for ref, plus in ((out_d, 1 - plus_c), (out_c, plus_c)):
        copies.append((density.at[plus, pl.ds(6 * plus, 7)], ref))
    copies += [(near_in, near), (pick_in, pick), (mask_in, mask)]
    made = [pltpu.make_async_copy(s, d, sems.at[i]) for i, (s, d) in enumerate(copies)]
    for copy in made:
        copy.start()
    for copy in made:
        copy.wait()


def put(ref, slot, value, pair):
    label = (pair.within * 13 + pair.offset).astype(f32)
    ref[slot, pl.ds(0, BASIS)] = value
    ref[slot, pl.ds(BASIS, EDGE)] = jnp.full((EDGE, BASIS), label, f32).astype(bf16)


def cross_kernel(
    near_in, pick_in, mask_in, source, density,
    out_b, out_d, out_a, out_c, inside, blocks, whole,
    near, pick, mask, queue, state, upto, home, held, int_sems, whole_sem, home_sem, sems,
):
    center = pltpu.make_async_copy(density.at[:, 6], home, home_sem)
    center.start()
    fetch_ints((near_in, pick_in, mask_in), (near, pick, mask), int_sems)
    for i in range(8):
        state[i] = 0

    def demand(t, length):
        pair = Pair(t, near, pick, mask)
        for other in (pair.k, pair.j):
            index = 4 * pair.g + other
            fresh = jnp.logical_and(state[index] == 0, pair.active)

            @pl.when(fresh)
            def _():
                queue[length] = index
                state[index] = 1

            length = length + jnp.where(fresh, 1, 0)
        upto[t] = length
        return length

    length = lax.fori_loop(0, 8, demand, 0)

    def load(q, carry):
        @pl.when(q < length)
        def _():
            index = queue[q]
            g, j = index // 4, lax.rem(index, 4)
            pltpu.make_async_copy(source.at[g, j], blocks.at[g, j], sems.at[index]).start()

        return carry

    def arrive(q, carry):
        pltpu.make_async_copy(source.at[0, 0], blocks.at[0, 0], sems.at[queue[q]]).wait()
        return load(q + FLIGHT, carry)

    lax.fori_loop(0, FLIGHT, load, 0)
    copy = pltpu.make_async_copy(density, whole, whole_sem)
    copy.start()
    for ref in (out_b, out_d, out_a, out_c, inside):
        ref[...] = jnp.zeros_like(ref)
    center.wait()

    def store(pair, value):
        value = value.astype(bf16)
        g, shift = pair.g, pair.shift
        slot = jnp.where(pair.reach > 0, 3 * g + shift - 2, g - shift - 1)
        slot = jnp.clip(slot, 0, 3)

        @pl.when(pair.reach == 0)
        def _():
            put(inside, jnp.clip(3 * g + shift, 0, 3), value, pair)

        @pl.when(pair.in_a)
        def _():
            put(out_a, slot, value, pair)

        @pl.when(pair.in_b)
        def _():
            put(out_b, slot, value, pair)

        @pl.when(pair.in_c)
        def _():
            put(out_c, 0, value, pair)

        @pl.when(pair.in_d)
        def _():
            put(out_d, 0, value, pair)

    def visit(i, arrived):
        pair = Pair(i, near, pick, mask)
        g, j, k = pair.g, pair.j, pair.k
        lax.fori_loop(arrived, upto[i], arrive, 0)

        @pl.when(pair.active)
        def _():
            store(pair, right_cross(home[g], blocks.at[g, k], blocks.at[g, j], held))

        return upto[i]

    lax.fori_loop(0, 8, visit, 0)
    copy.wait()


def own_kernel(
    far_b, far_d, far_a, far_c, near_in, pick_in, mask_in, blocks, whole, own,
    near, pick, mask, held, far, int_sems,
):
    fetch_ints((near_in, pick_in, mask_in), (near, pick, mask), int_sems)
    own[...] = jnp.zeros_like(own)

    def visit(i, carry):
        pair = Pair(i, near, pick, mask)
        g, j, k = pair.g, pair.j, pair.k

        @pl.when(pair.active)
        def _():
            start = jnp.where(pair.reach > 0, 1 - pair.within, 5 - pair.within)
            index = jnp.clip(pair.within * 8 + pair.offset - start, 0, 15)
            single = jnp.clip(pair.offset - 6 * (1 - pair.ahead), 0, 6)

            @pl.when(pair.reach == 0)
            def _():
                far[...] = whole[pair.within, pair.offset]

            @pl.when(pair.in_a)
            def _():
                far[...] = far_a[index]

            @pl.when(pair.in_b)
            def _():
                far[...] = far_b[index]

            @pl.when(pair.in_c)
            def _():
                far[...] = far_c[single]

            @pl.when(pair.in_d)
            def _():
                far[...] = far_d[single]

            own[g] += left_own(far[...], blocks.at[g, k], blocks.at[g, j], held)

        return carry

    lax.fori_loop(0, 8, visit, 0)


def rows_kernel(in_d, in_b, in_a, in_c, in_l, own, *outs):
    side = lax.axis_index("aux")
    for step, out in enumerate(outs):
        start = pl.multiple_of(lax.rem(side + step + 1, 4) * ROWS, ROWS)
        at = 0
        for ref in (in_b, in_d, in_a, in_c, in_l):
            for slot in range(1 if ref is in_c or ref is in_d else 4):
                out[at] = ref[slot, pl.ds(start, ROWS)]
                at += 1
        for g in range(2):
            out[at] = own[g, pl.ds(start, ROWS)].astype(bf16)
            at += 1


def band_kernel(in_d, in_b, in_a, in_c, in_l, own, from_1, from_2, from_3, band):
    side = lax.axis_index("aux")
    start = pl.multiple_of(side * ROWS, ROWS)
    band[...] = jnp.zeros_like(band)

    def others(at):
        return (
            from_1[at].astype(f32) + from_2[at].astype(f32) + from_3[at].astype(f32)
        )

    at = 0
    found = []
    for ref in (in_b, in_d, in_a, in_c, in_l):
        for slot in range(1 if ref is in_c or ref is in_d else 4):
            label = jnp.max(ref[slot, pl.ds(BASIS, EDGE)].astype(f32)).astype(jnp.int32)
            value = ref[slot, pl.ds(start, ROWS)].astype(f32) + others(at)
            found.append((jnp.clip(label, 0, 25), value))
            at += 1
    for g in range(2):
        found.append((13 * g + 6, own[g, pl.ds(start, ROWS)] + others(at)))
        at += 1
    for label, value in found:
        band[label] += value


def shape(*dims, dtype=bf16):
    return jax.ShapeDtypeStruct(dims, dtype)


def int_scratch():
    return [pltpu.SMEM((2, 4), jnp.int32)] * 3


def local(three_index, density, neighbours, partner, block_mask):
    limit = pltpu.CompilerParams(vmem_limit_bytes=8 << 20)
    small = pltpu.CompilerParams(vmem_limit_bytes=4 << 20)
    three_index, density, neighbours, partner, block_mask = [
        pltpu.with_memory_space_constraint(x, pltpu.HBM)
        for x in (three_index, density, neighbours, partner, block_mask)
    ]
    ints = (neighbours, partner, block_mask)
    dma = pltpu.SemaphoreType.DMA
    packed = pl.pallas_call(
        pack_kernel,
        in_specs=[ANY] * 4,
        out_specs=[VM] * 7,
        out_shape=[shape(n, 128, 128) for n in (16, 7, 16, 7)]
        + [pltpu.VMEM((2, 4), jnp.int32)] * 3,
        scratch_shapes=[dma((9,))],
        compiler_params=small,
        name="pack",
    )(density, *ints)
    ints = packed[4:]
    far_b = swapped(packed[0], "b")
    far_d = swapped(packed[1], "d")
    far_a = swapped(packed[2], "a")
    far_c = swapped(packed[3], "c")

    tall = BASIS + EDGE
    held = pltpu.VMEM((40 * BASIS, BASIS), bf16)
    out_b, out_d, out_a, out_c, inside, blocks, whole = pl.pallas_call(
        cross_kernel,
        in_specs=[ANY] * 5,
        out_specs=[VM] * 7,
        out_shape=[
            shape(4, tall, 128),
            shape(4, tall, 128),
            shape(4, tall, 128),
            shape(4, tall, 128),
            shape(4, tall, 128),
            pltpu.VMEM(three_index.shape, bf16),
            pltpu.VMEM(density.shape, bf16),
        ],
        scratch_shapes=int_scratch()
        + [pltpu.SMEM((8,), jnp.int32)] * 3
        + [pltpu.VMEM((2, 128, 128), bf16), held, dma((3,)), dma(()), dma(()), dma((8,))],
        compiler_params=limit,
        name="cross",
    )(*ints, three_index, density)
    in_b = swapped(out_b, "b")
    in_d = swapped(out_d, "d")
    in_a = swapped(out_a, "a")
    in_c = swapped(out_c, "c")

    own = pl.pallas_call(
        own_kernel,
        in_specs=[VM] * 4 + [ANY] * 3 + [VM, VM],
        out_specs=VM,
        out_shape=shape(2, 128, 128, dtype=f32),
        scratch_shapes=int_scratch() + [held, pltpu.VMEM((128, 128), bf16), dma((3,))],
        compiler_params=limit,
        name="own",
    )(far_b, far_d, far_a, far_c, *ints, blocks, whole)

    arrived = (in_d, in_b, in_a, in_c, inside, own)
    sends = pl.pallas_call(
        rows_kernel,
        in_specs=[VM] * 6,
        out_specs=[VM] * 3,
        out_shape=[shape(16, ROWS, 128)] * 3,
        compiler_params=small,
        name="rows",
    )(*arrived)
    received = []
    for step, send in enumerate(sends):
        pairs = [(x, (x + step + 1) % 4) for x in range(4)]
        received.append(lax.ppermute(send, "aux", pairs))
    band = pl.pallas_call(
        band_kernel,
        in_specs=[VM] * 9,
        out_specs=VM,
        out_shape=shape(26, ROWS, 128, dtype=f32),
        compiler_params=small,
        name="band",
    )(*arrived, *received)
    return band.reshape(2, 13, ROWS, 128)


def solution(mesh):
    return jax.shard_map(
        local,
        mesh=mesh,
        in_specs=(
            P("sfc", None, "aux", None, None),
            P("sfc", None, None, None),
            P("sfc", None),
            P("sfc", None),
            P("sfc", None),
        ),
        out_specs=P("sfc", None, "aux", None),
        check_vma=False,
    )
```
